32 devices in a mesh: band: 4 (over y, x), pw: 8 (over z, core).
Axes of the slice: x: 2, y: 2, z: 4, core: 2. Of those that a mesh axis runs over, the one named last changes fastest.
Arguments:
- psi: float32 [2, 8, 16384], P(None, None, 'pw'), may hold values from -60 to 60
- energies: float32 [8], P('band'), may hold values from -2 to 0
- kinetic: float32 [16384], P('pw'), may hold values from 0.05 to 20
- vloc: float32 [128, 128, 128], P('pw'), may hold values from 0.5 to 2
- dv: float32 [128, 128, 128], P('pw'), may hold values from -5 to 5
- beta: float32 [2, 64, 16384], P(None, None, 'pw'), may hold values from -0.046875 to 0.046875
- nl_diag: float32 [64], replicated, may hold values from 1 to 10
- nl_coupling: float32 [64], replicated, may hold values from -4 to 4
- proj_counts: int32 [16], replicated, may hold values from 1 to 13, 64 in all
- pw_map: int32 [16384], P('pw'), may hold values from 0 to 16383, as said below
- stick_pos: int32 [1024], replicated, may hold values from 0 to 16383, as said below
Outputs:
- dpsi: float32 [2, 8, 16384], P(None, 'band', 'pw')
- residual: float32 [2, 8, 16384], P(None, 'band', 'pw')
- drho: float32 [128, 128, 128], P('pw', 'band')
The draws below stay inside these ranges and needn't reach their ends.
Inputs may be any that keep to these rules, and one draw needn't show every extreme that they name: `pw_map`: within each block of 2048 entries (the plane waves of one pw index) the values are distinct, and each block holds 0 and 16383. `stick_pos`: all values distinct; 0 and 16383 appear.
All inputs are finite; a program needn't handle non-finite values.
Results may differ from the reference program's by a relative error of at most 0.0003.
Values sent between devices are 32-bit elements; how exact they have to be, the bound alone decides.
A program may use at most 256 MiB of HBM per device.

```python
import math
import jax
import jax.numpy as jnp
import numpy as np
from jax import lax

NG = 128
COLS_DEV = 128
NPW_DEV = 2048
NATOM = 16
NPROJ = 64
ITERS = 2
NOCC = 8
PW = 16384
STICKS = 1024


def draw_psi(key, part):
    key_base, key_band, key_wave = jax.random.split(key, 3)
    band_scale = jnp.exp(jax.random.uniform(key_band, (1, NOCC, 1), jnp.float32, 0.0, math.log(10.0)))
    wave_scale = jnp.exp(jax.random.uniform(key_wave, (1, 1, PW), jnp.float32, 0.0, math.log(10.0)))
    base_values = jnp.clip(jax.random.normal(key_base, (2, NOCC, PW), jnp.float32), -5.0, 5.0)
    drawn = base_values * band_scale * wave_scale / 10.0
    return drawn


def draw_dv(key, part):
    drawn = jnp.clip(jax.random.normal(key, (NG, NG, NG), jnp.float32), -5.0, 5.0)
    return drawn


def draw_pw_map(key, part):
    block_count = PW // NPW_DEV
    keys_all = jax.random.split(key, block_count)
    upper = COLS_DEV * NG - 1

    def one_block(block_key):
        key_perm, key_order = jax.random.split(block_key)
        middle = jax.random.permutation(key_perm, upper - 1)[:NPW_DEV - 2] + 1
        chosen = jnp.concatenate([jnp.zeros((1,), jnp.int32), middle.astype(jnp.int32), jnp.full((1,), upper, jnp.int32)])
        return jax.random.permutation(key_order, chosen)
    return jax.vmap(one_block)(keys_all).reshape(PW).astype(jnp.int32)


def draw_stick_pos(key, part):
    key_perm, key_order = jax.random.split(key)
    upper = NG * NG - 1
    middle = jax.random.permutation(key_perm, upper - 1)[:STICKS - 2] + 1
    chosen = jnp.concatenate([jnp.zeros((1,), jnp.int32), middle.astype(jnp.int32), jnp.full((1,), upper, jnp.int32)])
    return jax.random.permutation(key_order, chosen).astype(jnp.int32)


def shard_levels(own_key, dims, cuts, low, largest):
    def one(position, parts):
        steps = jax.random.uniform(jax.random.fold_in(jax.random.fold_in(own_key, 6), position), (parts,), jnp.float32, low / len(cuts), largest / len(cuts))
        return jnp.repeat(jnp.exp(steps), dims[position] // parts).reshape((-1,) + (1,) * (len(dims) - position - 1))

    gain = one(*cuts[0])
    for cut in cuts[1:]:
        gain = gain * one(*cut)
    return gain


def split_up(number_of, total, bound, lean):
    weights = [(1 << 20) // math.isqrt(rank ** lean) + 1 for rank in range(2, number_of + 1)]
    spare, counts = total - bound - (number_of - 1), [1] * (number_of - 1)
    while spare > 0:
        candidates = [i for i in range(number_of - 1) if counts[i] < bound]
        mass, left = sum([weights[i] for i in candidates]), spare
        for i in candidates:
            more = min(bound - counts[i], max(1, left * weights[i] // mass), spare)
            counts[i] = counts[i] + more
            spare = spare - more
    return np.array([bound] + counts)


def ragged(rng, amount, total, most, slope):
    if amount == 2:
        one = jax.random.randint(rng, (), max(1, total - most), min(most, total - 1) + 1)
        return jnp.stack([one, total - one])
    lengths = jnp.asarray(split_up(amount, total, most, slope), jnp.int32)
    couples = (amount - 1) // 2
    source_of, taker = lengths[1:1 + 2 * couples:2], lengths[2:2 + 2 * couples:2]
    slack = jnp.minimum(source_of - 1, most - taker)
    passed = jax.random.randint(jax.random.fold_in(rng, 1), (couples,), 0, 1 << 20) % (slack + 1)
    lengths = lengths.at[1:1 + 2 * couples:2].set(source_of - passed).at[2:2 + 2 * couples:2].set(taker + passed)
    return lengths[jax.random.permutation(jax.random.fold_in(rng, 2), amount)]


def centred(stream_key, extent, scale, reach, shards=(), kind=jnp.bfloat16):
    values = scale * jax.random.normal(stream_key, extent, jnp.float32)
    if shards:
        values = values * shard_levels(stream_key, extent, shards, -0.22, 0.18)
    return jnp.clip(values, -reach, reach).astype(kind)


def setup_inputs(seed: int = 0) -> dict:
    seeds = jax.random.split(jax.random.key(seed), 12)
    return {
        "psi": draw_psi(jax.random.fold_in(seeds[11], 71), 0),
        "energies": jnp.clip(-2.0 + 2.0 * jax.random.uniform(seeds[1], (NOCC,), jnp.float32) ** shard_levels(seeds[1], (NOCC,), ((0, 4),), -0.2, 0.2), -2.0, 0.0),
        "kinetic": jnp.clip(jnp.exp(math.log(20.0) - 5.9914645 * jax.random.uniform(seeds[2], (PW,), jnp.float32) ** shard_levels(seeds[2], (PW,), ((0, 8),), -0.2, 0.2)), 0.05, 20.0),
        "vloc": jnp.clip(0.5 + 1.5 * jax.random.uniform(seeds[3], (NG, NG, NG), jnp.float32) ** shard_levels(seeds[3], (NG, NG, NG), ((0, 8),), -0.2, 0.2), 0.5, 2.0),
        "dv": draw_dv(jax.random.fold_in(seeds[11], 71), 0),
        "beta": centred(seeds[5], (2, NPROJ, PW), PW ** -0.5, 0.046875, ((2, 8),), jnp.float32),
        "nl_diag": jnp.clip(jnp.exp(jax.random.uniform(seeds[6], (NPROJ,), jnp.float32, math.log(1.0), math.log(10.0))), 1.0, 10.0),
        "nl_coupling": centred(seeds[7], (NPROJ,), 1.0, 4.0, (), jnp.float32),
        "proj_counts": ragged(seeds[8], NATOM, NPROJ, 13, 0).astype(jnp.int32),
        "pw_map": draw_pw_map(jax.random.fold_in(seeds[11], 71), 0),
        "stick_pos": draw_stick_pos(jax.random.fold_in(seeds[11], 71), 0),
    }


PRECISE = lax.Precision.HIGHEST
ALPHA_SHIFT = 4.0

def grid_index(pw_map, stick_pos):
    device = jnp.arange(PW, dtype=jnp.int32) // NPW_DEV
    column = pw_map % COLS_DEV
    freq_z = pw_map // COLS_DEV
    stick = device * COLS_DEV + column
    return (freq_z * (NG * NG) + stick_pos[stick]).astype(jnp.int32)

def inverse_one(coeffs, flat_grid):
    volume = NG * NG * NG
    real_grid = jnp.zeros((volume,), coeffs.dtype).at[flat_grid].set(coeffs[0])
    imag_grid = jnp.zeros((volume,), coeffs.dtype).at[flat_grid].set(coeffs[1])
    field = lax.complex(real_grid, imag_grid).reshape(NG, NG, NG)
    return jnp.fft.ifftn(field) * math.sqrt(volume)

def forward_one(field, flat_grid):
    volume = NG * NG * NG
    spectrum = (jnp.fft.fftn(field) / math.sqrt(volume)).reshape(-1)[flat_grid]
    return jnp.stack([jnp.real(spectrum), jnp.imag(spectrum)])

def local_apply(coeffs, potential, flat_grid):
    by_band = jnp.transpose(coeffs, (1, 0, 2))
    result = lax.map(lambda single: forward_one(potential * inverse_one(single, flat_grid), flat_grid), by_band)
    return jnp.transpose(result, (1, 0, 2))

def project_onto(basis, vector):

    def product(left, right):
        return jnp.einsum('kg,ng->kn', left, right, precision=PRECISE)
    return jnp.stack([product(basis[0], vector[0]) + product(basis[1], vector[1]), product(basis[0], vector[1]) - product(basis[1], vector[0])])

def expand(basis, weights):

    def product(left, right):
        return jnp.einsum('kn,kg->ng', left, right, precision=PRECISE)
    return jnp.stack([product(weights[0], basis[0]) - product(weights[1], basis[1]), product(weights[0], basis[1]) + product(weights[1], basis[0])])

def dot_bands(left, right):
    return lax.optimization_barrier(jnp.sum(left * right, axis=(0, 2)))

def reference(psi, energies, kinetic, vloc, dv, beta, nl_diag, nl_coupling, proj_counts, pw_map, stick_pos):
    flat_grid = grid_index(pw_map, stick_pos)
    block_ends = jnp.cumsum(proj_counts).astype(jnp.int32)
    proj_index = jnp.arange(NPROJ, dtype=jnp.int32)
    atom_of = lax.optimization_barrier(jnp.sum((proj_index[:, None] >= block_ends[None, :]).astype(jnp.int32), axis=1))
    same_atom = (atom_of[:, None] == atom_of[None, :]).astype(jnp.float32)

    def couple(beta_proj):
        weighted = nl_coupling[None, :, None] * beta_proj
        grouped = jnp.einsum('ij,cjn->cin', same_atom, weighted, precision=PRECISE)
        return nl_diag[None, :, None] * beta_proj + nl_coupling[None, :, None] * grouped
    diagonal_shift = kinetic[None, None, :] - energies[None, :, None]
    precond = 1.0 / (1.0 + diagonal_shift)

    def operator(vector):
        local_part = local_apply(vector, vloc, flat_grid)
        nonlocal_part = expand(beta, couple(project_onto(beta, vector)))
        occupied_part = ALPHA_SHIFT / PW * expand(psi, project_onto(psi, vector))
        return diagonal_shift * vector + local_part + nonlocal_part + occupied_part
    dvpsi = local_apply(psi, dv, flat_grid)
    rhs = -(dvpsi - expand(psi, project_onto(psi, dvpsi)) / PW)
    solution = jnp.zeros_like(rhs)
    residual = rhs
    search = precond * residual
    norm_now = dot_bands(residual, search)
    for iteration in range(ITERS):
        image = operator(search)
        step_len = norm_now / dot_bands(search, image)
        solution = solution + step_len[None, :, None] * search
        residual = residual - step_len[None, :, None] * image
        if iteration + 1 < ITERS:
            precond_res = precond * residual
            norm_next = dot_bands(residual, precond_res)
            search = precond_res + (norm_next / norm_now)[None, :, None] * search
            norm_now = norm_next
    density_scale = 2.0 * NG * NG * NG / PW

    def add_band(total, pair):
        state_field = inverse_one(pair[0], flat_grid)
        change_field = inverse_one(pair[1], flat_grid)
        term = jnp.real(state_field) * jnp.real(change_field) + jnp.imag(state_field) * jnp.imag(change_field)
        return (total + density_scale * term, None)
    drho, _ = lax.scan(add_band, jnp.zeros((NG, NG, NG), jnp.float32), (jnp.transpose(psi, (1, 0, 2)), jnp.transpose(solution, (1, 0, 2))))
    return (solution, residual, drho)
```

```python
import functools
import math

import jax
import jax.numpy as jnp
import numpy as np
from jax import lax
from jax.experimental import pallas as pl
from jax.experimental.pallas import tpu as pltpu
from jax.sharding import PartitionSpec as P

ITERS = 2
PRECISE = lax.Precision.HIGH
ALPHA_SHIFT = 4.0
UNROLL = 16
KY_BLOCK = 32


def split(value):
    high = value.astype(jnp.bfloat16)
    return high, (value - high.astype(jnp.float32)).astype(jnp.bfloat16)


def dot32(left, right):
    return jnp.dot(left, right, preferred_element_type=jnp.float32)


def data_table(value, table_ref):
    high, low = split(value)
    return dot32(high, table_ref[0]) + dot32(low, table_ref[0]) + dot32(high, table_ref[1])


def table_data(table_ref, value):
    high, low = split(value)
    return dot32(table_ref[0], high) + dot32(table_ref[0], low) + dot32(table_ref[1], high)


def block_tables(length, scale):
    positions = np.arange(length)
    angles = (positions[:, None] * positions[None, :] % length) * (2.0 * math.pi / length)
    cosine, sine = np.cos(angles) * scale, np.sin(angles) * scale
    inverse_right = np.block([[cosine, sine], [-sine, cosine]])
    forward_right = np.block([[cosine, -sine], [sine, cosine]])
    stacked = np.stack([inverse_right, forward_right, inverse_right.T, forward_right.T]).astype(np.float32)
    high = stacked.astype(jnp.bfloat16)
    low = (stacked - high.astype(np.float32)).astype(jnp.bfloat16)
    return jnp.asarray(np.stack([high, low], axis=1))


def plane_kernel(size, planes, bands, mode, pos_ref, rows_ref, pot_ref, table_ref, *rest):
    items = bands * planes
    if mode == "first":
        back_ref, field_ref, grid_ref, mid_ref = rest
    else:
        state_ref, back_ref, energy_ref, density_ref, grid_ref, mid_ref = rest
        energy_ref[...] = jnp.zeros_like(energy_ref)
    sticks = rows_ref.shape[0]
    zero_rows = 512

    def clear(step, carry):
        grid_ref[pl.ds(pl.multiple_of(step * zero_rows, zero_rows), zero_rows), :] = jnp.zeros(
            (zero_rows, 2 * items), jnp.float32
        )
        return carry

    lax.fori_loop(0, size * size // zero_rows, clear, 0)

    def put(step, carry):
        for offset in range(UNROLL):
            stick = step * UNROLL + offset
            grid_ref[pl.ds(pos_ref[stick], 1), :] = rows_ref[pl.ds(stick, 1), :]
        return carry

    lax.fori_loop(0, sticks // UNROLL, put, 0)

    def x_inverse(step, carry):
        parts = []
        for offset in range(KY_BLOCK):
            start = pl.multiple_of((step * KY_BLOCK + offset) * size, size)
            turned = grid_ref[pl.ds(start, size), :].T
            parts.append(jnp.concatenate([turned[:items], turned[items:]], axis=1))
        result = data_table(jnp.concatenate(parts, axis=0), table_ref.at[0])
        height = KY_BLOCK * items
        for half in range(2):
            mid_ref[half, pl.ds(pl.multiple_of(step * height, height), height), :] = result[
                :, half * size : (half + 1) * size
            ]
        return carry

    lax.fori_loop(0, size // KY_BLOCK, x_inverse, 0)

    def y_stage(plane, carry):
        loads = []
        for band in range(bands):
            where = pl.ds(band * planes + plane, size, stride=items)
            loads.append(jnp.concatenate([mid_ref[0, where, :], mid_ref[1, where, :]], axis=0))
        field = table_data(table_ref.at[2], jnp.concatenate(loads, axis=1))
        potential = pot_ref[plane]
        wide = jnp.concatenate([potential] * bands, axis=1)
        shaped = field * jnp.concatenate([wide, wide], axis=0)
        if mode == "first":
            field_ref[plane] = field
        else:
            product = field * state_ref[plane]
            total = product[:size] + product[size:]
            height = density_ref.shape[3]
            for band in range(bands):
                for slab in range(density_ref.shape[1]):
                    density_ref[band, slab, plane] = total[
                        slab * height : (slab + 1) * height, band * size : (band + 1) * size
                    ]
            energy = (field * shaped).reshape(2 * size // 8, 8, bands * size)
            energy_ref[...] += jnp.sum(energy, axis=0)
        spectrum = table_data(table_ref.at[3], shaped)
        for band in range(bands):
            where = pl.ds(band * planes + plane, size, stride=items)
            for half in range(2):
                mid_ref[half, where, :] = spectrum[
                    half * size : (half + 1) * size, band * size : (band + 1) * size
                ]
        return carry

    lax.fori_loop(0, planes, y_stage, 0, unroll=4)

    def x_forward(step, carry):
        height = KY_BLOCK * items
        where = pl.ds(pl.multiple_of(step * height, height), height)
        result = data_table(
            jnp.concatenate([mid_ref[0, where, :], mid_ref[1, where, :]], axis=1), table_ref.at[1]
        )
        for offset in range(KY_BLOCK):
            piece = result[offset * items : (offset + 1) * items]
            start = pl.multiple_of((step * KY_BLOCK + offset) * size, size)
            grid_ref[pl.ds(start, size), :] = jnp.concatenate(
                [piece[:, :size], piece[:, size:]], axis=0
            ).T
        return carry

    lax.fori_loop(0, size // KY_BLOCK, x_forward, 0)

    def take(step, carry):
        for offset in range(UNROLL):
            stick = step * UNROLL + offset
            back_ref[pl.ds(stick, 1), :] = grid_ref[pl.ds(pos_ref[stick], 1), :]
        return carry

    lax.fori_loop(0, sticks // UNROLL, take, 0)


def plane_call(mode, size, planes, bands, positions, rows, potential, tables, *state):
    items = bands * planes
    back = jax.ShapeDtypeStruct(rows.shape, jnp.float32)
    field = jax.ShapeDtypeStruct((planes, 2 * size, bands * size), jnp.float32)
    energy = jax.ShapeDtypeStruct((8, bands * size), jnp.float32)
    slabs = lax.axis_size("band")
    density = jax.ShapeDtypeStruct((bands, slabs, planes, size // slabs, size), jnp.float32)
    shapes = {"first": (back, field), "apply": (back, energy, density)}[mode]
    vmem = pl.BlockSpec(memory_space=pltpu.VMEM)
    return pl.pallas_call(
        functools.partial(plane_kernel, size, planes, bands, mode),
        out_shape=shapes,
        in_specs=[pl.BlockSpec(memory_space=pltpu.SMEM), vmem, vmem, vmem] + [vmem for _ in state],
        out_specs=tuple(vmem for _ in shapes),
        scratch_shapes=[
            pltpu.VMEM((size * size, 2 * items), jnp.float32),
            pltpu.VMEM((2, size * items, size), jnp.float32),
        ],
        compiler_params=pltpu.CompilerParams(vmem_limit_bytes=48 * 2**20),
        name="plane_" + mode,
    )(positions, rows, potential, tables, *state)


def project_onto(basis, vector):
    def product(left, right):
        return jnp.einsum("kg,ng->kn", left, right, precision=PRECISE)

    return jnp.stack(
        [
            product(basis[0], vector[0]) + product(basis[1], vector[1]),
            product(basis[0], vector[1]) - product(basis[1], vector[0]),
        ]
    )


def expand(basis, weights):
    def product(left, right):
        return jnp.einsum("kn,kg->ng", left, right, precision=PRECISE)

    return jnp.stack(
        [
            product(weights[0], basis[0]) - product(weights[1], basis[1]),
            product(weights[0], basis[1]) + product(weights[1], basis[0]),
        ]
    )


def dot_bands(left, right):
    return jnp.sum(left * right, axis=(0, 2))


def shards(
    psi, energies, kinetic, vloc, dv, beta, nl_diag, nl_coupling, proj_counts, pw_map, stick_pos
):
    size = vloc.shape[1]
    plane_count = vloc.shape[0]
    groups = lax.axis_size("pw")
    columns = stick_pos.shape[0] // groups
    total_pw = kinetic.shape[0] * groups
    bands = energies.shape[0]
    padded = plane_count
    while bands * padded % 8:
        padded += 1
    norm_scale = 1.0 / math.sqrt(size**3)
    tables = block_tables(size, 1.0)
    own_states = lax.dynamic_slice_in_dim(psi, lax.axis_index("band") * bands, bands, 1)
    atoms = jnp.arange(proj_counts.shape[0], dtype=jnp.int32)
    block_ends = jnp.sum(
        jnp.where(atoms[None, :] <= atoms[:, None], proj_counts[None, :], 0), axis=1
    )
    proj_index = jnp.arange(beta.shape[1], dtype=jnp.int32)
    atom_of = jnp.sum((proj_index[:, None] >= block_ends[None, :]).astype(jnp.int32), axis=1)
    same_atom = (atom_of[:, None] == atom_of[None, :]).astype(jnp.float32)

    grid_points = np.arange(size)
    angles = (grid_points[:, None] * grid_points[None, :] % size) * (2.0 * math.pi / size)
    both = norm_scale * np.concatenate([np.cos(angles), np.sin(angles)]).astype(np.float32)
    both_high = both.astype(jnp.bfloat16)
    both_low = (both - both_high.astype(np.float32)).astype(jnp.bfloat16)
    level = (
        jnp.arange(size, dtype=jnp.int32)[:, None] == (pw_map // columns)[None, :]
    ).astype(jnp.bfloat16)
    phases = jnp.dot(both_high, level, preferred_element_type=jnp.float32) + jnp.dot(
        both_low, level, preferred_element_type=jnp.float32
    )
    cos_zg, sin_zg = phases[:size], phases[size:]
    pick = (
        jnp.arange(columns, dtype=jnp.int32)[:, None] == (pw_map % columns)[None, :]
    ).astype(jnp.bfloat16)

    def halves(value):
        high = lax.reduce_precision(value, 8, 7)
        return high.astype(jnp.bfloat16), (value - high).astype(jnp.bfloat16)

    def selected(form, value, chooser):
        high, low = halves(value)
        return jnp.einsum(form, high, chooser, preferred_element_type=jnp.float32) + jnp.einsum(
            form, low, chooser, preferred_element_type=jnp.float32
        )

    def exchange(blocks, carried):
        lanes = blocks.shape[2]
        extra = -(-carried.shape[0] // lanes)
        extra += -extra % 8
        tail = jnp.pad(carried, (0, extra * lanes - carried.shape[0])).reshape(1, extra, lanes)
        tail = jnp.broadcast_to(tail, (groups, extra, lanes))
        moved = lax.all_to_all(
            jnp.concatenate([blocks, tail], axis=1), "pw", split_axis=0, concat_axis=0, tiled=True
        )
        total = jnp.sum(moved[:, columns:], axis=0).reshape(-1)
        return moved[:, :columns], total[: carried.shape[0]]

    def group_sum(value):
        flat = value.reshape(-1)
        height = -(-flat.shape[0] // 1024) * 8
        flat = jnp.pad(flat, (0, height * 128 - flat.shape[0])).reshape(1, height, 128)
        moved = lax.all_to_all(
            jnp.broadcast_to(flat, (groups, height, 128)), "pw", split_axis=0, concat_axis=0, tiled=True
        )
        return jnp.sum(moved, axis=0).reshape(-1)[: value.size].reshape(value.shape)

    def to_rows(coeffs, carried):
        real, imag = coeffs[0][:, None, :], coeffs[1][:, None, :]
        turned = jnp.stack(
            [real * cos_zg - imag * sin_zg, imag * cos_zg + real * sin_zg]
        )
        sticks = selected("cbzg,sg->cbzs", turned, pick)
        sticks = sticks.reshape(2, bands, groups, plane_count, columns)
        sticks = jnp.transpose(sticks, (2, 4, 0, 1, 3)).reshape(groups, columns, -1)
        if carried is None:
            rows = lax.all_to_all(sticks, "pw", split_axis=0, concat_axis=0, tiled=True)
            total = None
        else:
            rows, total = exchange(sticks, carried)
        rows = rows.reshape(groups * columns, 2, bands, plane_count)
        rows = jnp.pad(rows, ((0, 0), (0, 0), (0, 0), (0, padded - plane_count)))
        return rows.reshape(groups * columns, -1), total

    def from_rows(rows, carried):
        rows = rows.reshape(groups * columns, 2, bands, padded)[..., :plane_count]
        rows = rows.reshape(groups, columns, -1)
        if carried is None:
            sticks = lax.all_to_all(rows, "pw", split_axis=0, concat_axis=0, tiled=True)
            total = None
        else:
            sticks, total = exchange(rows, carried)
        sticks = sticks.reshape(groups, columns, 2, bands, plane_count)
        sticks = jnp.transpose(sticks, (2, 3, 0, 4, 1)).reshape(2, bands, size, columns)
        chosen = selected("cbzs,sg->cbzg", sticks, pick)
        coeffs = jnp.stack(
            [
                jnp.sum(chosen[0] * cos_zg + chosen[1] * sin_zg, axis=1),
                jnp.sum(chosen[1] * cos_zg - chosen[0] * sin_zg, axis=1),
            ]
        )
        return coeffs, total

    def pad_planes(value):
        return jnp.pad(value, ((0, padded - plane_count), (0, 0), (0, 0)))

    def couple(beta_proj):
        weighted = nl_coupling[None, :, None] * beta_proj
        grouped = jnp.einsum("ij,cjn->cin", same_atom, weighted, precision=PRECISE)
        return nl_diag[None, :, None] * beta_proj + nl_coupling[None, :, None] * grouped

    def send_vector(vector, residual):
        parts = (project_onto(psi, vector), project_onto(beta, vector), dot_bands(residual, vector))
        rows, total = to_rows(vector, jnp.concatenate([part.reshape(-1) for part in parts]))
        first = parts[0].size
        second = first + parts[1].size
        return (
            rows,
            total[:first].reshape(parts[0].shape),
            total[first:second].reshape(parts[1].shape),
            total[second:],
        )

    def weigh(steps, density):
        return sum(steps[band] * density[band, :, :plane_count] for band in range(bands))

    diagonal_shift = kinetic[None, None, :] - energies[None, :, None]
    precond = 1.0 / (1.0 + diagonal_shift)
    state_rows, _ = to_rows(own_states, None)
    back, state_planes = plane_call(
        "first", size, padded, bands, stick_pos, state_rows, pad_planes(dv), tables
    )
    dvpsi, _ = from_rows(back, None)
    rhs_state = group_sum(project_onto(psi, dvpsi))
    rhs = -(dvpsi - expand(psi, rhs_state) / total_pw)
    solution = jnp.zeros_like(rhs)
    residual = rhs
    search = precond * residual
    rows, state_proj, beta_proj, norm_now = send_vector(search, residual)
    local_potential = pad_planes(vloc)
    density_scale = 2.0 * size**3 / total_pw
    weighed = []
    for iteration in range(ITERS):
        local_back, energy, density = plane_call(
            "apply", size, padded, bands, stick_pos, rows, local_potential, tables, state_planes
        )
        coupled = couple(beta_proj)
        nonlocal_part = expand(beta, coupled)
        occupied_part = ALPHA_SHIFT / total_pw * expand(psi, state_proj)
        known_part = diagonal_shift * search + nonlocal_part + occupied_part
        own_energy = jnp.sum(energy.reshape(8, bands, size), axis=(0, 2))
        own_energy = own_energy + dot_bands(search, diagonal_shift * search)
        local_part, curvature = from_rows(local_back, own_energy)
        curvature = curvature + jnp.sum(beta_proj * coupled, axis=(0, 1))
        curvature = curvature + ALPHA_SHIFT / total_pw * jnp.sum(state_proj * state_proj, axis=(0, 1))
        image = known_part + local_part
        step_len = norm_now / curvature
        solution = solution + step_len[None, :, None] * search
        residual = residual - step_len[None, :, None] * image
        weighed.append((density_scale * step_len, density))
        if iteration + 1 < ITERS:
            precond_res = precond * residual
            new_rows, new_state, new_beta, norm_next = send_vector(precond_res, residual)
            ratio = norm_next / norm_now
            lanes = jnp.broadcast_to(ratio[None, :, None], (2, bands, padded)).reshape(-1)
            rows = new_rows + lanes[None, :] * rows
            state_proj = new_state + ratio * state_proj
            beta_proj = new_beta + ratio * beta_proj
            search = precond_res + ratio[None, :, None] * search
            norm_now = norm_next
    density_term = sum(weigh(steps, density) for steps, density in weighed)
    drho = jnp.sum(
        lax.all_to_all(density_term, "band", split_axis=0, concat_axis=0, tiled=True), axis=0
    )
    return (solution, residual, drho)


def solution(mesh):
    placed = (
        P(None, None, "pw"),
        P("band"),
        P("pw"),
        P("pw", None, None),
        P("pw", None, None),
        P(None, None, "pw"),
        P(),
        P(),
        P(),
        P("pw"),
        P(),
    )
    return jax.shard_map(
        shards,
        mesh=mesh,
        in_specs=placed,
        out_specs=(P(None, "band", "pw"), P(None, "band", "pw"), P("pw", "band", None)),
        check_vma=False,
    )
```
